32 devices in a mesh: row: 4 (over x, core), col: 4 (over z), layer: 2 (over y).
Axes of the slice: x: 2, y: 2, z: 4, core: 2. Of those that a mesh axis runs over, the one named last changes fastest.
Arguments:
- a_values: float32 [32, 4, 2, 1, 64, 384], P('row', 'col', 'layer'), may hold values from -0.3125 to 0.3125
- a_columns: int32 [32, 4, 2, 1, 6], P('row', 'col', 'layer'), may hold values from 0 to 15
- b_values: float32 [64, 4, 2, 64, 512], P('row', 'col', 'layer'), may hold values from -6 to 6
- b_columns: int32 [64, 4, 2, 8], P('row', 'col', 'layer'), may hold values from 0 to 31
- keep_columns: int32 [32, 4, 4], P('row', 'col'), may hold values from 0 to 31
Outputs:
- kept_blocks: float32 [32, 4, 64, 256], P(('row', 'layer'), 'col')
The draws below stay inside these ranges and needn't reach their ends.
All inputs are finite; a program needn't handle non-finite values.
Results may differ from the reference program's by a relative error of at most 0.0003.
Values sent between devices are 32-bit elements; how exact they have to be, the bound alone decides.
A program may use at most 64 MiB of HBM per device.

```python
import jax
import jax.numpy as jnp
from jax import lax

BLK = 64
ROWB = 8
KROWB = 16
COLB = 32
SLOTS_A = 6
SLOTS_B = 8
KEEP = 4
GRID_ROWS = 4
GRID_COLS = 4
LAYERS = 2
IMAGES = 1
NRB = 32
NKB = 64


def with_ends(entries, rng, smallest, largest):
    shape = entries.shape
    index_at = [jax.random.randint(jax.random.fold_in(rng, axis), (), 0, shape[axis]) for axis in range(len(shape))]
    entries = entries.at[tuple(index_at)].set(smallest)
    longest = shape.index(max(shape))
    index_at[longest] = (index_at[longest] + 1) % shape[longest]
    return entries.at[tuple(index_at)].set(largest)


def level_of(key, dims, cuts, smallest, largest):
    def one(dim, shards_of):
        heights = jax.random.uniform(jax.random.fold_in(jax.random.fold_in(key, 6), dim), (shards_of,), jnp.float32, smallest / len(cuts), largest / len(cuts))
        return jnp.repeat(jnp.exp(heights), dims[dim] // shards_of).reshape((-1,) + (1,) * (len(dims) - dim - 1))

    gain = one(*cuts[0])
    for cut in cuts[1:]:
        gain = gain * one(*cut)
    return gain


def normal_values(rng, shape, scale, reach, split=(), kind=jnp.bfloat16):
    entries = scale * jax.random.normal(rng, shape, jnp.float32)
    if split:
        entries = entries * level_of(rng, shape, split, -0.22, 0.18)
    return jnp.clip(entries, -reach, reach).astype(kind)


def setup_inputs(seed: int = 0) -> dict:
    key_list = jax.random.split(jax.random.key(seed), 6)
    a_values = normal_values(key_list[0], (NRB, GRID_COLS, LAYERS, IMAGES, BLK, SLOTS_A * BLK), (BLK * SLOTS_A) ** -0.5, 0.3125, ((0, 4), (1, 4), (2, 2)), jnp.float32)
    a_columns = with_ends(jax.random.randint(key_list[1], (NRB, GRID_COLS, LAYERS, IMAGES, SLOTS_A), 0, KROWB), jax.random.fold_in(key_list[1], 1), 0, KROWB - 1).astype(jnp.int32)
    b_values = normal_values(key_list[2], (NKB, GRID_COLS, LAYERS, BLK, SLOTS_B * BLK), 1.0, 6.0, ((0, 4), (1, 4), (2, 2)), jnp.float32)
    b_columns = with_ends(jax.random.randint(key_list[3], (NKB, GRID_COLS, LAYERS, SLOTS_B), 0, COLB), jax.random.fold_in(key_list[3], 1), 0, COLB - 1).astype(jnp.int32)
    keep_columns = with_ends(jax.random.randint(key_list[4], (NRB, GRID_COLS, KEEP), 0, COLB), jax.random.fold_in(key_list[4], 1), 0, COLB - 1).astype(jnp.int32)
    return dict(a_values=a_values, a_columns=a_columns, b_values=b_values, b_columns=b_columns, keep_columns=keep_columns)


def block_term(left_values, left_index, right_values, right_index, keep_list):
    row_count = left_values.shape[0]
    blocks = left_values.reshape(row_count, BLK, SLOTS_A, BLK)
    gathered = jnp.take(right_values, left_index, axis=0)
    products = jnp.einsum('iawb,iwbv->iwav', blocks, gathered, precision=lax.Precision.HIGHEST)
    targets = jnp.take(right_index, left_index, axis=0)
    matches = (targets[:, :, :, None] == keep_list[:, None, None, :]).astype(jnp.float32)
    products = products.reshape(row_count, SLOTS_A, BLK, SLOTS_B, BLK)
    result = jnp.einsum('iwvu,iwavc->iauc', matches, products, precision=lax.Precision.HIGHEST)
    return result.reshape(row_count, BLK, KEEP * BLK)


def panel_term(left_values, left_index, right_values, right_index, keep_list):
    row_count = left_values.shape[0]
    groups = row_count // 4

    def group_term(pieces):
        return block_term(pieces[0], pieces[1], right_values, right_index, pieces[2])

    grouped = lax.map(group_term, (left_values.reshape(groups, 4, BLK, SLOTS_A * BLK), left_index.reshape(groups, 4, SLOTS_A), keep_list.reshape(groups, 4, KEEP)))
    return grouped.reshape(row_count, BLK, KEEP * BLK)


def reference(a_values, a_columns, b_values, b_columns, keep_columns):
    left = a_values.reshape(GRID_ROWS, ROWB, GRID_COLS, LAYERS, IMAGES, BLK, SLOTS_A * BLK)
    left_index = a_columns.reshape(GRID_ROWS, ROWB, GRID_COLS, LAYERS, IMAGES, SLOTS_A)
    right = b_values.reshape(GRID_ROWS, KROWB, GRID_COLS, LAYERS, BLK, SLOTS_B * BLK)
    right_index = b_columns.reshape(GRID_ROWS, KROWB, GRID_COLS, LAYERS, SLOTS_B)
    keep_panels = keep_columns.reshape(GRID_ROWS, ROWB, GRID_COLS, KEEP)

    def panel_at(position):
        grid_row = position // GRID_COLS
        grid_column = position % GRID_COLS

        def layer_section(running, layer_index):
            for section in range(2):
                contraction = (grid_row + grid_column + section) % GRID_ROWS
                image = contraction // GRID_COLS
                shifted_column = (grid_column + section) % GRID_COLS
                shifted_row = (grid_row + section) % GRID_ROWS
                running = running + panel_term(left[grid_row, :, shifted_column, layer_index, image], left_index[grid_row, :, shifted_column, layer_index, image], right[shifted_row, :, grid_column, layer_index], right_index[shifted_row, :, grid_column, layer_index], keep_panels[grid_row, :, grid_column])
            return running, None

        initial = jnp.zeros((ROWB, BLK, KEEP * BLK), jnp.float32)
        running, _ = lax.scan(layer_section, initial, jnp.arange(LAYERS, dtype=jnp.int32))
        return running

    panels = lax.map(panel_at, jnp.arange(GRID_ROWS * GRID_COLS, dtype=jnp.int32))
    panels = panels.reshape(GRID_ROWS, GRID_COLS, ROWB, BLK, KEEP * BLK).transpose(0, 2, 1, 3, 4)
    return panels.reshape(GRID_ROWS * ROWB, GRID_COLS, BLK, KEEP * BLK)
```

```python
import functools

import jax
import jax.numpy as jnp
from jax import lax
from jax.experimental import pallas as pl
from jax.experimental.pallas import tpu as pltpu
from jax.sharding import PartitionSpec as P

BLK = 64
SLOTS_A = 6
SLOTS_B = 8
KEEP = 4
LANES = 128
OWN_AT, SENT_AT, KEEP_AT, TARGET_AT = 0, 8, 16, 24


def kernel(
    sizes,
    a_hbm, b_hbm, ints_v, ints_s,
    out,
    own_a, far_a, b, rolled, targets, term0, term1, got0, got1,
    far_cols_v, far_keep_v, far_cols, far_keep,
    load_sem, a_send, a_recv, int_send, int_recv, int_load,
    send0, recv0, send1, recv1,
):
    grid_rows, grid_cols, layers = sizes
    rows = own_a.shape[0]
    krows = b.shape[0]
    share = rows // layers
    r, c, l = lax.axis_index("row"), lax.axis_index("col"), lax.axis_index("layer")
    up, down = lax.rem(r + 1, grid_rows), lax.rem(r + grid_rows - 1, grid_rows)
    right, left = lax.rem(c + 1, grid_cols), lax.rem(c + grid_cols - 1, grid_cols)

    barrier = pltpu.get_barrier_semaphore()
    partners = [(up, left, l), (down, right, l)]
    for other in range(layers):
        partners += [(up, c, other), (down, c, other)]
    for step in range(1, layers):
        partners.append((r, c, lax.rem(l + step, layers)))
    for partner in partners:
        pl.semaphore_signal(barrier, inc=1, device_id=partner, device_id_type=pl.DeviceIdType.MESH)

    own_image = lax.rem(r + c, grid_rows) // grid_cols
    sent_image = lax.rem(r + left + 1, grid_rows) // grid_cols
    load_b = pltpu.make_async_copy(b_hbm.at[:, 0, 0], b, load_sem.at[0])
    load_a = pltpu.make_async_copy(a_hbm.at[:, 0, 0, own_image], own_a, load_sem.at[1])
    load_b.start()
    load_a.start()
    pl.semaphore_wait(barrier, len(partners))

    def remote(src, dst, sent, received, target):
        return pltpu.make_async_remote_copy(
            src_ref=src, dst_ref=dst, send_sem=sent, recv_sem=received,
            device_id=target, device_id_type=pl.DeviceIdType.MESH,
        )

    move_cols = remote(ints_v, far_cols_v, int_send.at[0], int_recv.at[0], (up, left, l))
    move_keep = remote(ints_v, far_keep_v, int_send.at[1], int_recv.at[1], (up, c, l))
    move_cols.start()
    move_keep.start()

    def row_at(step):
        return lax.rem(step, layers) * share + step // layers

    def move_a(step):
        i = row_at(step)
        return remote(
            a_hbm.at[i, 0, 0, sent_image], far_a.at[i], a_send.at[i], a_recv.at[i], (up, left, l)
        )

    for step in range(rows):
        move_a(step).start()

    low = lax.broadcasted_iota(jnp.int32, (8, LANES), 1) < BLK
    load_b.wait()

    def prepare(k, carry):
        for pair in range(SLOTS_B // 2):
            cut = slice(pair * LANES, (pair + 1) * LANES)
            rolled[k, :, cut] = pltpu.roll(b[k, :, cut], BLK, 1)
            first = ints_s[k, TARGET_AT + 2 * pair]
            second = ints_s[k, TARGET_AT + 2 * pair + 1]
            targets[k, 2 * pair] = jnp.where(low, first, second)
            targets[k, 2 * pair + 1] = jnp.where(low, second, first)
        return carry

    lax.fori_loop(0, krows, prepare, 0)

    def row_term(a_row, i, cols, cols_at, keep):
        kept = [
            jnp.where(low, keep[i, KEEP_AT + 2 * half], keep[i, KEEP_AT + 2 * half + 1])
            for half in range(KEEP // 2)
        ]
        a_high = a_row.astype(jnp.bfloat16)
        a_low = (a_row - a_high.astype(jnp.float32)).astype(jnp.bfloat16)
        a_both = jnp.concatenate([a_high, a_low], axis=0)
        total = None
        for first in range(0, SLOTS_A, 2):
            picked = []
            for w in (first, first + 1):
                k = cols[i, cols_at + w]
                sums = [None] * (KEEP // 2)
                for slot in range(SLOTS_B):
                    cut = slice(slot // 2 * LANES, (slot // 2 + 1) * LANES)
                    source = b if slot % 2 == 0 else rolled
                    block = source[k, :, cut].reshape(BLK // 8, 8, LANES)
                    target = targets[k, slot]
                    for half in range(KEEP // 2):
                        mask = jnp.broadcast_to((target == kept[half])[None], block.shape)
                        part = jnp.where(mask, block, 0.0)
                        sums[half] = part if sums[half] is None else sums[half] + part
                picked.append(jnp.concatenate([s.reshape(BLK, LANES) for s in sums], axis=1))
            g = jnp.concatenate(picked, axis=0)
            g_high = g.astype(jnp.bfloat16)
            g_low = (g - g_high.astype(jnp.float32)).astype(jnp.bfloat16)
            cut = slice(first * BLK, (first + 2) * BLK)
            both = jnp.dot(a_both[:, cut], g_high, preferred_element_type=jnp.float32)
            part = both[:BLK] + both[BLK:] + jnp.dot(
                a_high[:, cut], g_low, preferred_element_type=jnp.float32
            )
            total = part if total is None else total + part
        return total

    def move_term0(i):
        return remote(
            term0.at[i], got0.at[l, lax.rem(i, share)], send0.at[i],
            recv0.at[l, lax.rem(i, share)], (r, c, i // share)
        )

    def move_term1(i):
        return remote(
            term1.at[i], got1.at[l, lax.rem(i, share)], send1.at[i],
            recv1.at[l, lax.rem(i, share)], (down, c, i // share)
        )

    load_a.wait()

    def other_rows(step, carry):
        i = lax.rem((l + 1) * share + step, rows)
        term0[i] = row_term(own_a[i], i, ints_s, OWN_AT, ints_s)
        move_term0(i).start()
        return carry

    def own_rows(step, carry):
        i = l * share + step
        term0[i] = row_term(own_a[i], i, ints_s, OWN_AT, ints_s)
        return carry

    lax.fori_loop(0, rows - share, other_rows, 0)
    lax.fori_loop(0, share, own_rows, 0)

    move_cols.wait_recv()
    move_keep.wait_recv()
    load_cols = pltpu.make_async_copy(far_cols_v, far_cols, int_load.at[0])
    load_keep = pltpu.make_async_copy(far_keep_v, far_keep, int_load.at[1])
    load_cols.start()
    load_keep.start()
    load_cols.wait()
    load_keep.wait()

    def far_rows(step, carry):
        i = row_at(step)
        move_a(step).wait_recv()
        term1[i] = row_term(far_a[i], i, far_cols, SENT_AT, far_keep)
        move_term1(i).start()
        return carry

    lax.fori_loop(0, rows, far_rows, 0)

    def final(j, carry):
        total = term0[l * share + j]
        for step in range(1, layers):
            other = lax.rem(l + step, layers)
            remote(term0.at[0], got0.at[other, j], send0.at[0], recv0.at[other, j], (r, c, other)).wait_recv()
            total = total + got0[other, j]
        for other in range(layers):
            remote(term1.at[0], got1.at[other, j], send1.at[0], recv1.at[other, j], (up, c, other)).wait_recv()
            total = total + got1[other, j]
        out[j, 0] = total
        return carry

    lax.fori_loop(0, share, final, 0)

    move_cols.wait_send()
    move_keep.wait_send()

    def sent_other(step, carry):
        move_term0(lax.rem((l + 1) * share + step, rows)).wait_send()
        return carry

    def sent_rows(i, carry):
        move_a(i).wait_send()
        move_term1(i).wait_send()
        return carry

    lax.fori_loop(0, rows - share, sent_other, 0)
    lax.fori_loop(0, rows, sent_rows, 0)


def per_device(a_values, a_columns, b_values, b_columns, keep_columns):
    sizes = tuple(lax.axis_size(name) for name in ("row", "col", "layer"))
    grid_rows, grid_cols, layers = sizes
    rows, krows = a_values.shape[0], b_values.shape[0]
    share = rows // layers
    r, c = lax.axis_index("row"), lax.axis_index("col")
    receiver = (c + grid_cols - 1) % grid_cols
    all_index = a_columns[:, 0, 0]
    own = lax.dynamic_index_in_dim(all_index, (r + c) % grid_rows // grid_cols, 1, keepdims=False)
    sent = lax.dynamic_index_in_dim(all_index, (r + receiver + 1) % grid_rows // grid_cols, 1, keepdims=False)

    def placed(x, at):
        return jnp.pad(x, ((0, krows - x.shape[0]), (at, LANES - at - x.shape[1])))

    ints = (
        placed(own, OWN_AT) + placed(sent, SENT_AT)
        + placed(keep_columns[:, 0], KEEP_AT) + placed(b_columns[:, 0, 0], TARGET_AT)
    )
    width = KEEP * BLK
    depth = SLOTS_A * BLK
    f32, i32 = jnp.float32, jnp.int32
    dma = pltpu.SemaphoreType.DMA
    return pl.pallas_call(
        functools.partial(kernel, sizes),
        out_shape=jax.ShapeDtypeStruct((share, 1, BLK, width), f32),
        in_specs=[
            pl.BlockSpec(memory_space=pl.ANY),
            pl.BlockSpec(memory_space=pl.ANY),
            pl.BlockSpec(memory_space=pltpu.VMEM),
            pl.BlockSpec(memory_space=pltpu.SMEM),
        ],
        out_specs=pl.BlockSpec(memory_space=pltpu.VMEM),
        scratch_shapes=[
            pltpu.VMEM((rows, BLK, depth), f32),
            pltpu.VMEM((rows, BLK, depth), f32),
            pltpu.VMEM((krows, BLK, SLOTS_B * BLK), f32),
            pltpu.VMEM((krows, BLK, SLOTS_B * BLK), f32),
            pltpu.VMEM((krows, SLOTS_B, 8, LANES), i32),
            pltpu.VMEM((rows, BLK, width), f32),
            pltpu.VMEM((rows, BLK, width), f32),
            pltpu.VMEM((layers, share, BLK, width), f32),
            pltpu.VMEM((layers, share, BLK, width), f32),
            pltpu.VMEM((krows, LANES), i32),
            pltpu.VMEM((krows, LANES), i32),
            pltpu.SMEM((krows, LANES), i32),
            pltpu.SMEM((krows, LANES), i32),
            dma((2,)), dma((rows,)), dma((rows,)), dma((2,)), dma((2,)), dma((2,)),
            dma((rows,)), dma((layers, share)), dma((rows,)), dma((layers, share)),
        ],
        compiler_params=pltpu.CompilerParams(
            collective_id=0, has_side_effects=True, vmem_limit_bytes=32 * 1024 * 1024
        ),
    )(a_values, b_values, ints, ints)


def solution(mesh):
    placed = (
        P("row", "col", "layer", None, None, None),
        P("row", "col", "layer", None, None),
        P("row", "col", "layer", None, None),
        P("row", "col", "layer", None),
        P("row", "col", None),
    )
    return jax.shard_map(
        per_device,
        mesh=mesh,
        in_specs=placed,
        out_specs=P(("row", "layer"), "col", None, None),
        check_vma=False,
    )
```

```python
import functools

import jax
import jax.numpy as jnp
from jax import lax
from jax.experimental import pallas as pl
from jax.experimental.pallas import tpu as pltpu
from jax.sharding import PartitionSpec as P

BLK = 64
SLOTS_A = 6
SLOTS_B = 8
KEEP = 4
LANES = 128


def kernel(
    sizes,
    a_hbm, b_hbm, cols_hbm, keep_hbm, targets_hbm,
    out,
    own_a, far_a, b, rolled, targets, g_high, g_low, term0, term1, got0, got1,
    own_cols, own_keep, own_targets, far_cols_v, far_keep_v, far_cols, far_keep,
    load_sem, a_send, a_recv, int_send, int_recv, int_load,
    send0, recv0, send1, recv1,
):
    grid_rows, grid_cols, layers = sizes
    rows = own_a.shape[0]
    krows = b.shape[0]
    share = rows // layers
    r, c, l = lax.axis_index("row"), lax.axis_index("col"), lax.axis_index("layer")
    up, down = lax.rem(r + 1, grid_rows), lax.rem(r + grid_rows - 1, grid_rows)
    right, left = lax.rem(c + 1, grid_cols), lax.rem(c + grid_cols - 1, grid_cols)

    barrier = pltpu.get_barrier_semaphore()
    senders = [(down, right, l), (down, c, l)]
    senders += [(up, c, other) for other in range(layers)]
    senders += [(r, c, lax.rem(l + step, layers)) for step in range(1, layers)]
    for partner in senders:
        pl.semaphore_signal(barrier, inc=1, device_id=partner, device_id_type=pl.DeviceIdType.MESH)

    own_image = lax.rem(r + c, grid_rows) // grid_cols
    sent_image = lax.rem(r + left + 1, grid_rows) // grid_cols
    load_b = pltpu.make_async_copy(b_hbm.at[:, 0, 0], b, load_sem.at[0])
    load_a = pltpu.make_async_copy(a_hbm.at[:, 0, 0, own_image], own_a, load_sem.at[1])
    load_ints = [
        pltpu.make_async_copy(src, dst, load_sem.at[2 + at])
        for at, (src, dst) in enumerate(
            [(cols_hbm, own_cols), (keep_hbm, own_keep), (targets_hbm, own_targets)]
        )
    ]
    load_b.start()
    load_a.start()
    for load in load_ints:
        load.start()
    pl.semaphore_wait(barrier, len(senders))

    def remote(src, dst, sent, received, target):
        return pltpu.make_async_remote_copy(
            src_ref=src, dst_ref=dst, send_sem=sent, recv_sem=received,
            device_id=target, device_id_type=pl.DeviceIdType.MESH,
        )

    move_cols = remote(cols_hbm, far_cols_v, int_send.at[0], int_recv.at[0], (up, left, l))
    move_keep = remote(keep_hbm, far_keep_v, int_send.at[1], int_recv.at[1], (up, c, l))
    move_cols.start()
    move_keep.start()

    def row_at(step):
        return lax.rem(step, layers) * share + step // layers

    def move_a(step):
        i = row_at(step)
        return remote(
            a_hbm.at[i, 0, 0, sent_image], far_a.at[i], a_send.at[i], a_recv.at[i], (up, left, l)
        )

    for step in range(rows):
        move_a(step).start()

    low = lax.broadcasted_iota(jnp.int32, (8, LANES), 1) < BLK
    load_b.wait()
    for load in load_ints:
        load.wait()

    def prepare(k, carry):
        for pair in range(SLOTS_B // 2):
            cut = slice(pair * LANES, (pair + 1) * LANES)
            rolled[k, :, cut] = pltpu.roll(b[k, :, cut], BLK, 1)
            first = own_targets[2 * pair, k]
            second = own_targets[2 * pair + 1, k]
            targets[k, 2 * pair] = jnp.where(low, first, second)
            targets[k, 2 * pair + 1] = jnp.where(low, second, first)
        return carry

    lax.fori_loop(0, krows, prepare, 0)

    def gather(i, cols, keep):
        kept = [
            jnp.where(low, keep[2 * half, i], keep[2 * half + 1, i])
            for half in range(KEEP // 2)
        ]
        for w in range(SLOTS_A):
            k = cols[w, own_image, i]
            sums = [None] * (KEEP // 2)
            for slot in range(SLOTS_B):
                cut = slice(slot // 2 * LANES, (slot // 2 + 1) * LANES)
                source = b if slot % 2 == 0 else rolled
                block = source[k, :, cut].reshape(BLK // 8, 8, LANES)
                target = targets[k, slot]
                for half in range(KEEP // 2):
                    mask = jnp.broadcast_to((target == kept[half])[None], block.shape)
                    part = jnp.where(mask, block, 0.0)
                    sums[half] = part if sums[half] is None else sums[half] + part
            g = jnp.concatenate([s.reshape(BLK, LANES) for s in sums], axis=1)
            high = g.astype(jnp.bfloat16)
            g_high[i, w * BLK:(w + 1) * BLK, :] = high
            g_low[i, w * BLK:(w + 1) * BLK, :] = (g - high.astype(jnp.float32)).astype(jnp.bfloat16)

    def multiply(a_row, i):
        a_high = a_row.astype(jnp.bfloat16)
        a_low = (a_row - a_high.astype(jnp.float32)).astype(jnp.bfloat16)
        both = jnp.dot(
            jnp.concatenate([a_high, a_low], axis=0), g_high[i], preferred_element_type=jnp.float32
        )
        return both[:BLK] + both[BLK:] + jnp.dot(
            a_high, g_low[i], preferred_element_type=jnp.float32
        )

    def move_term0(i):
        return remote(
            term0.at[i], got0.at[l, lax.rem(i, share)], send0.at[i],
            recv0.at[l, lax.rem(i, share)], (r, c, i // share)
        )

    def move_term1(i):
        return remote(
            term1.at[i], got1.at[l, lax.rem(i, share)], send1.at[i],
            recv1.at[l, lax.rem(i, share)], (down, c, i // share)
        )

    load_a.wait()

    def other_rows(step, carry):
        i = lax.rem((l + 1) * share + step, rows)
        gather(i, own_cols, own_keep)
        term0[i] = multiply(own_a[i], i)
        move_term0(i).start()
        return carry

    def own_rows(step, carry):
        i = l * share + step
        gather(i, own_cols, own_keep)
        term0[i] = multiply(own_a[i], i)
        return carry

    lax.fori_loop(0, rows - share, other_rows, 0)
    lax.fori_loop(0, share, own_rows, 0)

    move_cols.wait_recv()
    move_keep.wait_recv()
    load_cols = pltpu.make_async_copy(far_cols_v, far_cols, int_load.at[0])
    load_keep = pltpu.make_async_copy(far_keep_v, far_keep, int_load.at[1])
    load_cols.start()
    load_keep.start()
    load_cols.wait()
    load_keep.wait()

    def far_gather(i, carry):
        gather(i, far_cols, far_keep)
        return carry

    lax.fori_loop(0, rows, far_gather, 0)

    def far_rows(step, carry):
        i = row_at(step)
        move_a(step).wait_recv()
        term1[i] = multiply(far_a[i], i)
        move_term1(i).start()
        return carry

    lax.fori_loop(0, rows, far_rows, 0)

    def final(j, carry):
        total = term0[l * share + j]
        for step in range(1, layers):
            other = lax.rem(l + step, layers)
            remote(term0.at[0], got0.at[other, j], send0.at[0], recv0.at[other, j], (r, c, other)).wait_recv()
            total = total + got0[other, j]
        for other in range(layers):
            remote(term1.at[0], got1.at[other, j], send1.at[0], recv1.at[other, j], (up, c, other)).wait_recv()
            total = total + got1[other, j]
        out[j, 0] = total
        return carry

    lax.fori_loop(0, share, final, 0)

    move_cols.wait_send()
    move_keep.wait_send()

    def sent_other(step, carry):
        move_term0(lax.rem((l + 1) * share + step, rows)).wait_send()
        return carry

    def sent_rows(i, carry):
        move_a(i).wait_send()
        move_term1(i).wait_send()
        return carry

    lax.fori_loop(0, rows - share, sent_other, 0)
    lax.fori_loop(0, rows, sent_rows, 0)


def per_device(a_values, a_columns, b_values, b_columns, keep_columns):
    sizes = tuple(lax.axis_size(name) for name in ("row", "col", "layer"))
    layers = sizes[2]
    rows, krows = a_values.shape[0], b_values.shape[0]
    share = rows // layers
    cols = jnp.transpose(a_columns[:, 0, 0], (2, 1, 0))
    keep = jnp.transpose(keep_columns[:, 0])
    targets = jnp.transpose(b_columns[:, 0, 0])
    width = KEEP * BLK
    depth = SLOTS_A * BLK
    f32, i32 = jnp.float32, jnp.int32
    dma = pltpu.SemaphoreType.DMA
    return pl.pallas_call(
        functools.partial(kernel, sizes),
        out_shape=jax.ShapeDtypeStruct((share, 1, BLK, width), f32),
        in_specs=[
            pl.BlockSpec(memory_space=pltpu.HBM),
            pl.BlockSpec(memory_space=pltpu.HBM),
            pl.BlockSpec(memory_space=pltpu.HBM),
            pl.BlockSpec(memory_space=pltpu.HBM),
            pl.BlockSpec(memory_space=pltpu.HBM),
        ],
        out_specs=pl.BlockSpec(memory_space=pltpu.VMEM),
        scratch_shapes=[
            pltpu.VMEM((rows, BLK, depth), f32),
            pltpu.VMEM((rows, BLK, depth), f32),
            pltpu.VMEM((krows, BLK, SLOTS_B * BLK), f32),
            pltpu.VMEM((krows, BLK, SLOTS_B * BLK), f32),
            pltpu.VMEM((krows, SLOTS_B, 8, LANES), i32),
            pltpu.VMEM((rows, depth, width), jnp.bfloat16),
            pltpu.VMEM((rows, depth, width), jnp.bfloat16),
            pltpu.VMEM((rows, BLK, width), f32),
            pltpu.VMEM((rows, BLK, width), f32),
            pltpu.VMEM((layers, share, BLK, width), f32),
            pltpu.VMEM((layers, share, BLK, width), f32),
            pltpu.SMEM(cols.shape, i32),
            pltpu.SMEM(keep.shape, i32),
            pltpu.SMEM(targets.shape, i32),
            pltpu.VMEM(cols.shape, i32),
            pltpu.VMEM(keep.shape, i32),
            pltpu.SMEM(cols.shape, i32),
            pltpu.SMEM(keep.shape, i32),
            dma((5,)), dma((rows,)), dma((rows,)), dma((2,)), dma((2,)), dma((2,)),
            dma((rows,)), dma((layers, share)), dma((rows,)), dma((layers, share)),
        ],
        compiler_params=pltpu.CompilerParams(
            collective_id=0, has_side_effects=True, vmem_limit_bytes=60 * 1024 * 1024
        ),
    )(a_values, b_values, cols, keep, targets)


def solution(mesh):
    placed = (
        P("row", "col", "layer", None, None, None),
        P("row", "col", "layer", None, None),
        P("row", "col", "layer", None, None),
        P("row", "col", "layer", None),
        P("row", "col", None),
    )
    return jax.shard_map(
        per_device,
        mesh=mesh,
        in_specs=placed,
        out_specs=P(("row", "layer"), "col", None, None),
        check_vma=False,
    )
```

```python
import functools

import jax
import jax.numpy as jnp
from jax import lax
from jax.experimental import pallas as pl
from jax.experimental.pallas import tpu as pltpu
from jax.sharding import PartitionSpec as P

BLK = 64
SLOTS_A = 6
SLOTS_B = 8
KEEP = 4
LANES = 128


def kernel(
    sizes,
    a_hbm, b_hbm, cols_hbm, keep_hbm, targets_hbm,
    out,
    own_a, far_a, b, rolled, targets, g_high, g_low, term0, term1, got0, got1,
    own_cols, own_keep, own_targets, far_cols_v, far_keep_v, far_cols, far_keep,
    load_sem, a_send, a_recv, int_send, int_recv, int_load,
    send0, recv0, send1, recv1,
):
    grid_rows, grid_cols, layers = sizes
    rows = own_a.shape[0]
    krows = b.shape[0]
    share = rows // layers
    r, c, l = lax.axis_index("row"), lax.axis_index("col"), lax.axis_index("layer")
    up, down = lax.rem(r + 1, grid_rows), lax.rem(r + grid_rows - 1, grid_rows)
    right, left = lax.rem(c + 1, grid_cols), lax.rem(c + grid_cols - 1, grid_cols)

    barrier = pltpu.get_barrier_semaphore()
    senders = [(down, right, l), (down, c, l)]
    senders += [(up, c, other) for other in range(layers)]
    senders += [(r, c, lax.rem(l + step, layers)) for step in range(1, layers)]
    for partner in senders:
        pl.semaphore_signal(barrier, inc=1, device_id=partner, device_id_type=pl.DeviceIdType.MESH)

    own_image = lax.rem(r + c, grid_rows) // grid_cols
    sent_image = lax.rem(r + left + 1, grid_rows) // grid_cols
    load_b = pltpu.make_async_copy(b_hbm.at[:, 0, 0], b, load_sem.at[0])
    load_a = pltpu.make_async_copy(a_hbm.at[:, 0, 0, own_image], own_a, load_sem.at[1])
    load_ints = [
        pltpu.make_async_copy(src, dst, load_sem.at[2 + at])
        for at, (src, dst) in enumerate(
            [(cols_hbm, own_cols), (keep_hbm, own_keep), (targets_hbm, own_targets)]
        )
    ]
    load_b.start()
    load_a.start()
    for load in load_ints:
        load.start()
    pl.semaphore_wait(barrier, len(senders))

    def remote(src, dst, sent, received, target):
        return pltpu.make_async_remote_copy(
            src_ref=src, dst_ref=dst, send_sem=sent, recv_sem=received,
            device_id=target, device_id_type=pl.DeviceIdType.MESH,
        )

    move_cols = remote(cols_hbm, far_cols_v, int_send.at[0], int_recv.at[0], (up, left, l))
    move_keep = remote(keep_hbm, far_keep_v, int_send.at[1], int_recv.at[1], (up, c, l))
    move_cols.start()
    move_keep.start()

    def row_at(step):
        return lax.rem(step, layers) * share + step // layers

    def move_a(step):
        i = row_at(step)
        return remote(
            a_hbm.at[i, 0, 0, sent_image], far_a.at[i], a_send.at[i], a_recv.at[i], (up, left, l)
        )

    for step in range(rows):
        move_a(step).start()

    low = lax.broadcasted_iota(jnp.int32, (8, LANES), 1) < BLK
    load_b.wait()
    for load in load_ints:
        load.wait()

    def prepare(k, carry):
        for pair in range(SLOTS_B // 2):
            cut = slice(pair * LANES, (pair + 1) * LANES)
            rolled[k, :, cut] = pltpu.roll(b[k, :, cut], BLK, 1)
            first = own_targets[2 * pair, k]
            second = own_targets[2 * pair + 1, k]
            targets[k, 2 * pair] = jnp.where(low, first, second)
            targets[k, 2 * pair + 1] = jnp.where(low, second, first)
        return carry

    lax.fori_loop(0, krows, prepare, 0)

    def gather(i, cols, keep):
        kept = [
            jnp.where(low, keep[2 * half, i], keep[2 * half + 1, i])
            for half in range(KEEP // 2)
        ]
        for w in range(SLOTS_A):
            k = cols[w, own_image, i]
            sums = [None] * (KEEP // 2)
            for slot in range(SLOTS_B):
                cut = slice(slot // 2 * LANES, (slot // 2 + 1) * LANES)
                source = b if slot % 2 == 0 else rolled
                block = source[k, :, cut].reshape(BLK // 8, 8, LANES)
                target = targets[k, slot]
                for half in range(KEEP // 2):
                    mask = jnp.broadcast_to((target == kept[half])[None], block.shape)
                    part = jnp.where(mask, block, 0.0)
                    sums[half] = part if sums[half] is None else sums[half] + part
            g = jnp.concatenate([s.reshape(BLK, LANES) for s in sums], axis=1)
            high = g.astype(jnp.bfloat16)
            g_high[i, w * BLK:(w + 1) * BLK, :] = high
            g_low[i, w * BLK:(w + 1) * BLK, :] = (g - high.astype(jnp.float32)).astype(jnp.bfloat16)

    def multiply(a_row, i):
        a_high = a_row.astype(jnp.bfloat16)
        a_low = (a_row - a_high.astype(jnp.float32)).astype(jnp.bfloat16)
        both = jnp.dot(
            jnp.concatenate([a_high, a_low], axis=0), g_high[i], preferred_element_type=jnp.float32
        )
        return both[:BLK] + both[BLK:] + jnp.dot(
            a_high, g_low[i], preferred_element_type=jnp.float32
        )

    def move_term0(i):
        return remote(
            term0.at[i], got0.at[l, lax.rem(i, share)], send0.at[i],
            recv0.at[l, lax.rem(i, share)], (r, c, i // share)
        )

    def move_term1(i):
        return remote(
            term1.at[i], got1.at[l, lax.rem(i, share)], send1.at[i],
            recv1.at[l, lax.rem(i, share)], (down, c, i // share)
        )

    load_a.wait()

    def other_rows(step, carry):
        i = lax.rem((l + 1) * share + step, rows)
        gather(i, own_cols, own_keep)
        term0[i] = multiply(own_a[i], i)
        move_term0(i).start()
        return carry

    def own_rows(step, carry):
        i = l * share + step
        gather(i, own_cols, own_keep)
        term0[i] = multiply(own_a[i], i)
        return carry

    lax.fori_loop(0, rows - share, other_rows, 0)
    lax.fori_loop(0, share, own_rows, 0)

    move_cols.wait_recv()
    move_keep.wait_recv()
    load_cols = pltpu.make_async_copy(far_cols_v, far_cols, int_load.at[0])
    load_keep = pltpu.make_async_copy(far_keep_v, far_keep, int_load.at[1])
    load_cols.start()
    load_keep.start()
    load_cols.wait()
    load_keep.wait()

    def far_gather(i, carry):
        gather(i, far_cols, far_keep)
        return carry

    lax.fori_loop(0, rows, far_gather, 0)

    def far_rows(step, carry):
        i = row_at(step)
        move_a(step).wait_recv()
        term1[i] = multiply(far_a[i], i)
        move_term1(i).start()
        return carry

    lax.fori_loop(0, rows, far_rows, 0)

    def final(j, carry):
        total = term0[l * share + j]
        for step in range(1, layers):
            other = lax.rem(l + step, layers)
            remote(term0.at[0], got0.at[other, j], send0.at[0], recv0.at[other, j], (r, c, other)).wait_recv()
            total = total + got0[other, j]
        for other in range(layers):
            remote(term1.at[0], got1.at[other, j], send1.at[0], recv1.at[other, j], (up, c, other)).wait_recv()
            total = total + got1[other, j]
        out[j, 0] = total
        return carry

    lax.fori_loop(0, share, final, 0)

    move_cols.wait_send()
    move_keep.wait_send()

    def sent_other(step, carry):
        move_term0(lax.rem((l + 1) * share + step, rows)).wait_send()
        return carry

    def sent_rows(i, carry):
        move_a(i).wait_send()
        move_term1(i).wait_send()
        return carry

    lax.fori_loop(0, rows - share, sent_other, 0)
    lax.fori_loop(0, rows, sent_rows, 0)


def per_device(a_values, a_columns, b_values, b_columns, keep_columns):
    sizes = tuple(lax.axis_size(name) for name in ("row", "col", "layer"))
    layers = sizes[2]
    rows, krows = a_values.shape[0], b_values.shape[0]
    share = rows // layers
    cols = jnp.transpose(a_columns[:, 0, 0], (2, 1, 0))
    keep = jnp.transpose(keep_columns[:, 0])
    targets = jnp.transpose(b_columns[:, 0, 0])
    width = KEEP * BLK
    depth = SLOTS_A * BLK
    f32, i32 = jnp.float32, jnp.int32
    dma = pltpu.SemaphoreType.DMA
    return pl.pallas_call(
        functools.partial(kernel, sizes),
        out_shape=jax.ShapeDtypeStruct((share, 1, BLK, width), f32),
        in_specs=[
            pl.BlockSpec(memory_space=pltpu.HBM),
            pl.BlockSpec(memory_space=pltpu.HBM),
            pl.BlockSpec(memory_space=pltpu.HBM),
            pl.BlockSpec(memory_space=pltpu.HBM),
            pl.BlockSpec(memory_space=pltpu.HBM),
        ],
        out_specs=pl.BlockSpec(memory_space=pltpu.VMEM),
        scratch_shapes=[
            pltpu.VMEM((rows, BLK, depth), f32),
            pltpu.VMEM((rows, BLK, depth), f32),
            pltpu.VMEM((krows, BLK, SLOTS_B * BLK), f32),
            pltpu.VMEM((krows, BLK, SLOTS_B * BLK), f32),
            pltpu.VMEM((krows, SLOTS_B, 8, LANES), i32),
            pltpu.VMEM((rows, depth, width), jnp.bfloat16),
            pltpu.VMEM((rows, depth, width), jnp.bfloat16),
            pltpu.VMEM((rows, BLK, width), f32),
            pltpu.VMEM((rows, BLK, width), f32),
            pltpu.VMEM((layers, share, BLK, width), f32),
            pltpu.VMEM((layers, share, BLK, width), f32),
            pltpu.SMEM(cols.shape, i32),
            pltpu.SMEM(keep.shape, i32),
            pltpu.SMEM(targets.shape, i32),
            pltpu.VMEM(cols.shape, i32),
            pltpu.VMEM(keep.shape, i32),
            pltpu.SMEM(cols.shape, i32),
            pltpu.SMEM(keep.shape, i32),
            dma((5,)), dma((rows,)), dma((rows,)), dma((2,)), dma((2,)), dma((2,)),
            dma((rows,)), dma((layers, share)), dma((rows,)), dma((layers, share)),
        ],
        compiler_params=pltpu.CompilerParams(
            collective_id=0, has_side_effects=True, vmem_limit_bytes=32 * 1024 * 1024
        ),
    )(*(pltpu.with_memory_space_constraint(x, pltpu.HBM) for x in (a_values, b_values, cols, keep, targets)))


def solution(mesh):
    placed = (
        P("row", "col", "layer", None, None, None),
        P("row", "col", "layer", None, None),
        P("row", "col", "layer", None, None),
        P("row", "col", "layer", None),
        P("row", "col", None),
    )
    return jax.shard_map(
        per_device,
        mesh=mesh,
        in_specs=placed,
        out_specs=P(("row", "layer"), "col", None, None),
        check_vma=False,
    )
```

```python
import functools

import jax
import jax.numpy as jnp
from jax import lax
from jax.experimental import pallas as pl
from jax.experimental.pallas import tpu as pltpu
from jax.sharding import PartitionSpec as P

BLK = 64
SLOTS_A = 6
SLOTS_B = 8
KEEP = 4
LANES = 128


def kernel(
    sizes,
    a_hbm, b_hbm, cols_hbm, keep_hbm, targets_hbm,
    out,
    own_a, far_a, b, rolled, targets, g_high, g_low, term0, term1, got0, got1,
    own_cols, own_keep, own_targets, far_cols_v, far_keep_v, far_cols, far_keep,
    load_sem, a_send, a_recv, int_send, int_recv, int_load,
    send0, recv0, send1, recv1,
):
    grid_rows, grid_cols, layers = sizes
    rows = own_a.shape[0]
    krows = b.shape[0]
    share = rows // layers
    r, c, l = lax.axis_index("row"), lax.axis_index("col"), lax.axis_index("layer")
    up, down = lax.rem(r + 1, grid_rows), lax.rem(r + grid_rows - 1, grid_rows)
    right, left = lax.rem(c + 1, grid_cols), lax.rem(c + grid_cols - 1, grid_cols)

    barrier = pltpu.get_barrier_semaphore()
    senders = [(down, right, l), (down, c, l)]
    senders += [(up, c, other) for other in range(layers)]
    senders += [(r, c, lax.rem(l + step, layers)) for step in range(1, layers)]
    for partner in senders:
        pl.semaphore_signal(barrier, inc=1, device_id=partner, device_id_type=pl.DeviceIdType.MESH)

    own_image = lax.rem(r + c, grid_rows) // grid_cols
    sent_image = lax.rem(r + left + 1, grid_rows) // grid_cols
    load_b = pltpu.make_async_copy(b_hbm.at[:, 0, 0], b, load_sem.at[0])
    load_a = pltpu.make_async_copy(a_hbm.at[:, 0, 0, own_image], own_a, load_sem.at[1])
    load_ints = [
        pltpu.make_async_copy(src, dst, load_sem.at[2 + at])
        for at, (src, dst) in enumerate(
            [(cols_hbm, own_cols), (keep_hbm, own_keep), (targets_hbm, own_targets)]
        )
    ]
    for load in load_ints:
        load.start()
    pl.semaphore_wait(barrier, len(senders))

    def remote(src, dst, sent, received, target):
        return pltpu.make_async_remote_copy(
            src_ref=src, dst_ref=dst, send_sem=sent, recv_sem=received,
            device_id=target, device_id_type=pl.DeviceIdType.MESH,
        )

    move_cols = remote(cols_hbm, far_cols_v, int_send.at[0], int_recv.at[0], (up, left, l))
    move_keep = remote(keep_hbm, far_keep_v, int_send.at[1], int_recv.at[1], (up, c, l))
    move_cols.start()
    move_keep.start()

    def row_at(step):
        return lax.rem(step, layers) * share + step // layers

    def move_a(step):
        i = row_at(step)
        return remote(
            a_hbm.at[i, 0, 0, sent_image], far_a.at[i], a_send.at[i], a_recv.at[i], (up, left, l)
        )

    for step in range(rows):
        move_a(step).start()
    load_b.start()
    load_a.start()

    low = lax.broadcasted_iota(jnp.int32, (8, LANES), 1) < BLK
    load_b.wait()
    for load in load_ints:
        load.wait()

    def prepare(k, carry):
        for pair in range(SLOTS_B // 2):
            cut = slice(pair * LANES, (pair + 1) * LANES)
            rolled[k, :, cut] = pltpu.roll(b[k, :, cut], BLK, 1)
            first = own_targets[2 * pair, k]
            second = own_targets[2 * pair + 1, k]
            targets[k, 2 * pair] = jnp.where(low, first, second)
            targets[k, 2 * pair + 1] = jnp.where(low, second, first)
        return carry

    lax.fori_loop(0, krows, prepare, 0)

    def gather(i, cols, keep):
        kept = [
            jnp.where(low, keep[2 * half, i], keep[2 * half + 1, i])
            for half in range(KEEP // 2)
        ]
        for w in range(SLOTS_A):
            k = cols[w, own_image, i]
            sums = [None] * (KEEP // 2)
            for slot in range(SLOTS_B):
                cut = slice(slot // 2 * LANES, (slot // 2 + 1) * LANES)
                source = b if slot % 2 == 0 else rolled
                block = source[k, :, cut].reshape(BLK // 8, 8, LANES)
                target = targets[k, slot]
                for half in range(KEEP // 2):
                    mask = jnp.broadcast_to((target == kept[half])[None], block.shape)
                    part = jnp.where(mask, block, 0.0)
                    sums[half] = part if sums[half] is None else sums[half] + part
            g = jnp.concatenate([s.reshape(BLK, LANES) for s in sums], axis=1)
            high = g.astype(jnp.bfloat16)
            g_high[i, w * BLK:(w + 1) * BLK, :] = high
            g_low[i, w * BLK:(w + 1) * BLK, :] = (g - high.astype(jnp.float32)).astype(jnp.bfloat16)

    def multiply(a_row, i):
        a_high = a_row.astype(jnp.bfloat16)
        a_low = (a_row - a_high.astype(jnp.float32)).astype(jnp.bfloat16)
        both = jnp.dot(
            jnp.concatenate([a_high, a_low], axis=0), g_high[i], preferred_element_type=jnp.float32
        )
        return both[:BLK] + both[BLK:] + jnp.dot(
            a_high, g_low[i], preferred_element_type=jnp.float32
        )

    def move_term0(i):
        return remote(
            term0.at[i], got0.at[l, lax.rem(i, share)], send0.at[i],
            recv0.at[l, lax.rem(i, share)], (r, c, i // share)
        )

    def move_term1(i):
        return remote(
            term1.at[i], got1.at[l, lax.rem(i, share)], send1.at[i],
            recv1.at[l, lax.rem(i, share)], (down, c, i // share)
        )

    load_a.wait()

    def other_rows(step, carry):
        i = lax.rem((l + 1) * share + step, rows)
        gather(i, own_cols, own_keep)
        term0[i] = multiply(own_a[i], i)
        move_term0(i).start()
        return carry

    def own_rows(step, carry):
        i = l * share + step
        gather(i, own_cols, own_keep)
        term0[i] = multiply(own_a[i], i)
        return carry

    lax.fori_loop(0, rows - share, other_rows, 0)
    lax.fori_loop(0, share, own_rows, 0)

    move_cols.wait_recv()
    move_keep.wait_recv()
    load_cols = pltpu.make_async_copy(far_cols_v, far_cols, int_load.at[0])
    load_keep = pltpu.make_async_copy(far_keep_v, far_keep, int_load.at[1])
    load_cols.start()
    load_keep.start()
    load_cols.wait()
    load_keep.wait()

    def far_gather(i, carry):
        gather(i, far_cols, far_keep)
        return carry

    lax.fori_loop(0, rows, far_gather, 0)

    def early(j, carry):
        total = term0[l * share + j]
        for step in range(1, layers):
            other = lax.rem(l + step, layers)
            remote(term0.at[0], got0.at[other, j], send0.at[0], recv0.at[other, j], (r, c, other)).wait_recv()
            total = total + got0[other, j]
        out[j, 0] = total
        return carry

    lax.fori_loop(0, share, early, 0)

    def far_rows(step, carry):
        i = row_at(step)
        move_a(step).wait_recv()
        term1[i] = multiply(far_a[i], i)
        move_term1(i).start()
        return carry

    lax.fori_loop(0, rows, far_rows, 0)

    def final(j, carry):
        total = out[j, 0]
        for other in range(layers):
            remote(term1.at[0], got1.at[other, j], send1.at[0], recv1.at[other, j], (up, c, other)).wait_recv()
            total = total + got1[other, j]
        out[j, 0] = total
        return carry

    lax.fori_loop(0, share, final, 0)

    move_cols.wait_send()
    move_keep.wait_send()

    def sent_other(step, carry):
        move_term0(lax.rem((l + 1) * share + step, rows)).wait_send()
        return carry

    def sent_rows(i, carry):
        move_a(i).wait_send()
        move_term1(i).wait_send()
        return carry

    lax.fori_loop(0, rows - share, sent_other, 0)
    lax.fori_loop(0, rows, sent_rows, 0)


def per_device(a_values, a_columns, b_values, b_columns, keep_columns):
    sizes = tuple(lax.axis_size(name) for name in ("row", "col", "layer"))
    layers = sizes[2]
    rows, krows = a_values.shape[0], b_values.shape[0]
    share = rows // layers
    cols = jnp.transpose(a_columns[:, 0, 0], (2, 1, 0))
    keep = jnp.transpose(keep_columns[:, 0])
    targets = jnp.transpose(b_columns[:, 0, 0])
    width = KEEP * BLK
    depth = SLOTS_A * BLK
    f32, i32 = jnp.float32, jnp.int32
    dma = pltpu.SemaphoreType.DMA
    return pl.pallas_call(
        functools.partial(kernel, sizes),
        out_shape=jax.ShapeDtypeStruct((share, 1, BLK, width), f32),
        in_specs=[
            pl.BlockSpec(memory_space=pltpu.HBM),
            pl.BlockSpec(memory_space=pltpu.HBM),
            pl.BlockSpec(memory_space=pltpu.HBM),
            pl.BlockSpec(memory_space=pltpu.HBM),
            pl.BlockSpec(memory_space=pltpu.HBM),
        ],
        out_specs=pl.BlockSpec(memory_space=pltpu.VMEM),
        scratch_shapes=[
            pltpu.VMEM((rows, BLK, depth), f32),
            pltpu.VMEM((rows, BLK, depth), f32),
            pltpu.VMEM((krows, BLK, SLOTS_B * BLK), f32),
            pltpu.VMEM((krows, BLK, SLOTS_B * BLK), f32),
            pltpu.VMEM((krows, SLOTS_B, 8, LANES), i32),
            pltpu.VMEM((rows, depth, width), jnp.bfloat16),
            pltpu.VMEM((rows, depth, width), jnp.bfloat16),
            pltpu.VMEM((rows, BLK, width), f32),
            pltpu.VMEM((rows, BLK, width), f32),
            pltpu.VMEM((layers, share, BLK, width), f32),
            pltpu.VMEM((layers, share, BLK, width), f32),
            pltpu.SMEM(cols.shape, i32),
            pltpu.SMEM(keep.shape, i32),
            pltpu.SMEM(targets.shape, i32),
            pltpu.VMEM(cols.shape, i32),
            pltpu.VMEM(keep.shape, i32),
            pltpu.SMEM(cols.shape, i32),
            pltpu.SMEM(keep.shape, i32),
            dma((5,)), dma((rows,)), dma((rows,)), dma((2,)), dma((2,)), dma((2,)),
            dma((rows,)), dma((layers, share)), dma((rows,)), dma((layers, share)),
        ],
        compiler_params=pltpu.CompilerParams(
            collective_id=0, has_side_effects=True, vmem_limit_bytes=32 * 1024 * 1024
        ),
    )(*(pltpu.with_memory_space_constraint(x, pltpu.HBM) for x in (a_values, b_values, cols, keep, targets)))


def solution(mesh):
    placed = (
        P("row", "col", "layer", None, None, None),
        P("row", "col", "layer", None, None),
        P("row", "col", "layer", None, None),
        P("row", "col", "layer", None),
        P("row", "col", None),
    )
    return jax.shard_map(
        per_device,
        mesh=mesh,
        in_specs=placed,
        out_specs=P(("row", "layer"), "col", None, None),
        check_vma=False,
    )
```
